512 devices in a mesh: gx: 8 (over y), gy: 8 (over z_lo, core), gz: 8 (over z_hi, x).
Axes of the slice: x: 4, y: 8, z: 8 (z_hi: 2, z_lo: 4; z = z_hi * 4 + z_lo), core: 2. Of those that a mesh axis runs over, the one named last changes fastest.
Arguments:
- acts: bfloat16 [512, 12288], P(('gx', 'gy'), 'gz'), may hold values from -6 to 6
- grad_out: bfloat16 [512, 12288], P(('gx', 'gy'), 'gz'), may hold values from -3 to 3
- w_in: bfloat16 [12288, 24576], P('gz', ('gx', 'gy')), may hold values from -0.0546875 to 0.0546875
- b_in: float32 [24576], P(('gx', 'gy')), may hold values from -3 to 3
- w_out: bfloat16 [24576, 12288], P(('gx', 'gy'), 'gz'), may hold values from -0.0390625 to 0.0390625
Outputs:
- grad_acts: bfloat16 [512, 12288], P(('gx', 'gy'), 'gz')
- grad_w_in: bfloat16 [12288, 24576], P('gz', ('gx', 'gy'))
- grad_b_in: float32 [24576], P(('gx', 'gy'))
- grad_w_out: bfloat16 [24576, 12288], P(('gx', 'gy'), 'gz')
The draws below stay inside these ranges and needn't reach their ends.
All inputs are finite; a program needn't handle non-finite values.
Results may differ from the reference program's by a relative error of at most 0.007.
Values may be sent and summed in bfloat16 or wider, within the bound.
No kernel may reach another device: no remote copies, remote signals or barrier semaphores. Data moves between devices by JAX's collectives and lax.ppermute only.
A program may use at most 64 MiB of HBM per device.

```python
import jax
import jax.numpy as jnp
from jax import lax

D = 12288
FF = 24576
TOKENS = 512


def steps_of(own_key, dims, split, low, largest):
    level, own = 1.0, jax.random.fold_in(own_key, 6)
    for axis_at, blocks in split:
        draws = jnp.exp(jax.random.uniform(jax.random.fold_in(own, axis_at), (blocks,), jnp.float32, low / len(split), largest / len(split)))
        level = level * jnp.repeat(draws, dims[axis_at] // blocks).reshape([-1 if axis == axis_at else 1 for axis in range(len(dims))])
    return level


def normal_values(key, shape, scale, reach, pieces=(), kind=jnp.bfloat16):
    array = scale * jax.random.normal(key, shape, jnp.float32)
    if pieces:
        array = array * steps_of(key, shape, pieces, -0.22, 0.18)
    return jnp.clip(array, -reach, reach).astype(kind)


def setup_inputs(seed: int = 0) -> dict:
    key_of = jax.random.split(jax.random.key(seed), 6)
    acts = normal_values(key_of[0], (TOKENS, D), 1.0, 6.0, ((0, 64), (1, 8)))
    grad_out = normal_values(key_of[1], (TOKENS, D), 0.5, 3.0, ((0, 64), (1, 8)))
    w_in = normal_values(key_of[2], (D, FF), D ** -0.5, 0.0546875, ((0, 8), (1, 64)))
    b_in = normal_values(key_of[3], (FF,), 0.5, 3.0, ((0, 64),), jnp.float32)
    w_out = normal_values(key_of[4], (FF, D), FF ** -0.5, 0.0390625, ((0, 64), (1, 8)))
    return dict(acts=acts, grad_out=grad_out, w_in=w_in, b_in=b_in, w_out=w_out)


def activate(preact, back):
    cdf = 0.5 * (1.0 + lax.erf(preact * 0.7071067811865476))
    dens = jnp.exp(-0.5 * preact * preact) * 0.3989422804014327
    activation = (preact * cdf).astype(jnp.bfloat16)
    grad_pre = (back * (cdf + preact * dens)).astype(jnp.bfloat16)
    return activation, grad_pre


def reference(acts, grad_out, w_in, b_in, w_out):
    preact = jnp.dot(acts, w_in, preferred_element_type=jnp.float32) + b_in[None, :]
    back = jnp.dot(grad_out, w_out.T, preferred_element_type=jnp.float32)
    activation, grad_pre = activate(preact, back)
    grad_w_in = jnp.dot(acts.T, grad_pre, preferred_element_type=jnp.float32).astype(jnp.bfloat16)
    grad_b_in = jnp.sum(grad_pre.astype(jnp.float32), axis=0)
    grad_w_out = jnp.dot(activation.T, grad_out, preferred_element_type=jnp.float32).astype(jnp.bfloat16)
    grad_acts = jnp.dot(grad_pre, w_in.T, preferred_element_type=jnp.float32).astype(jnp.bfloat16)
    return grad_acts, grad_w_in, grad_b_in, grad_w_out
```

```python
import jax
import jax.numpy as jnp
from jax import lax
from jax.sharding import Mesh, PartitionSpec as P

BF16 = jnp.bfloat16
F32 = jnp.float32
PLANE = ("y", "zl")
MODEL = ("zh", "x")


def activate(preact, back):
    cdf = 0.5 * (1.0 + lax.erf(preact * 0.7071067811865476))
    dens = jnp.exp(-0.5 * preact * preact) * 0.3989422804014327
    activation = (preact * cdf).astype(BF16)
    grad_pre = (back * (cdf + preact * dens)).astype(BF16)
    return activation, grad_pre


def contract_rows(left, right):
    return lax.dot_general(
        left, right, (((0,), (0,)), ((), ())), preferred_element_type=F32
    )


def contract_cols(left, right):
    return lax.dot_general(
        left, right, (((1,), (1,)), ((), ())), preferred_element_type=F32
    )


def swap_cores(value):
    return lax.ppermute(value, "co", [(0, 1), (1, 0)])


def gather_blocks(value, axes):
    count = lax.axis_size(axes)
    copies = jnp.broadcast_to(value[None], (count, *value.shape))
    return lax.all_to_all(copies, axes, 0, 0, tiled=True)


def gather_tokens(value):
    own = gather_blocks(value, PLANE).reshape(-1, value.shape[1])
    return jnp.concatenate([own, swap_cores(own)], axis=0)


def sum_blocks(value, axes):
    count = lax.axis_size(axes)
    blocks = value.astype(BF16).reshape(count, value.shape[0] // count, value.shape[1])
    blocks = lax.all_to_all(blocks, axes, 0, 0, tiled=True)
    return jnp.sum(blocks.astype(F32), axis=0)


def body(acts, grad_out, w_in, b_in, w_out):
    inputs_all = gather_tokens(acts)
    outgrad_all = gather_tokens(grad_out)
    preact = sum_blocks(jnp.dot(inputs_all, w_in, preferred_element_type=F32), MODEL)
    back = sum_blocks(contract_cols(outgrad_all, w_out), MODEL)
    activation, grad_pre = activate(preact + b_in[None, :], back)
    width = b_in.shape[0]
    grad_pre = gather_blocks(grad_pre, MODEL).reshape(-1, width)
    activation = gather_blocks(activation, MODEL).reshape(-1, width)
    grad_w_in = contract_rows(inputs_all, grad_pre).astype(BF16)
    grad_b_in = jnp.sum(grad_pre.astype(F32), axis=0)
    grad_w_out = contract_rows(activation, outgrad_all).astype(BF16)
    partial = contract_cols(grad_pre, w_in)
    half = partial.shape[0] // 2
    partial = partial[:half] + swap_cores(partial[half:].astype(BF16)).astype(F32)
    grad_acts = sum_blocks(partial, PLANE).astype(BF16)
    return (grad_acts, grad_w_in, grad_b_in, grad_w_out)


def solution(mesh):
    fine = Mesh(mesh.devices.reshape(8, 4, 2, 2, 4), ("y", "zl", "co", "zh", "x"))
    tokens = ("y", "zl", "co")
    return jax.shard_map(
        body,
        mesh=fine,
        in_specs=(
            P(tokens, MODEL),
            P(tokens, MODEL),
            P(MODEL, tokens),
            P(tokens),
            P(tokens, MODEL),
        ),
        out_specs=(
            P(tokens, MODEL),
            P(MODEL, tokens),
            P(tokens),
            P(tokens, MODEL),
        ),
        check_vma=False,
    )
```

```python
import jax
import jax.numpy as jnp
from jax import lax
from jax.sharding import Mesh, PartitionSpec as P

BF16 = jnp.bfloat16
F32 = jnp.float32
PLANE = ("y", "zl")
MODEL = ("zh", "x")


def activate(preact, back):
    cdf = 0.5 * (1.0 + lax.erf(preact * 0.7071067811865476))
    dens = jnp.exp(-0.5 * preact * preact) * 0.3989422804014327
    activation = (preact * cdf).astype(BF16)
    grad_pre = (back * (cdf + preact * dens)).astype(BF16)
    return activation, grad_pre


def contract_rows(left, right):
    return lax.dot_general(
        left, right, (((0,), (0,)), ((), ())), preferred_element_type=F32
    )


def contract_cols(left, right):
    return lax.dot_general(
        left, right, (((1,), (1,)), ((), ())), preferred_element_type=F32
    )


def swap_cores(value):
    return lax.ppermute(value, "co", [(0, 1), (1, 0)])


def gather_blocks(value, axes):
    count = lax.axis_size(axes)
    copies = jnp.broadcast_to(value[None], (count, *value.shape))
    return lax.all_to_all(copies, axes, 0, 0, tiled=True).reshape(-1, value.shape[1])


def sum_blocks(value, axes):
    count = lax.axis_size(axes)
    blocks = value.reshape(count, value.shape[0] // count, value.shape[1])
    blocks = lax.all_to_all(blocks, axes, 0, 0, tiled=True)
    return jnp.sum(blocks.astype(F32), axis=0)


def sum_model(value):
    value = sum_blocks(value, "x").astype(BF16)
    other = lax.ppermute(value, "zh", [(0, 1), (1, 0)])
    return value.astype(F32) + other.astype(F32)


def body(acts, grad_out, w_in, b_in, w_out):
    width, hidden = w_in.shape
    own = gather_blocks(jnp.concatenate([acts, grad_out], axis=1), PLANE)
    both = jnp.concatenate([own, swap_cores(own)], axis=0)
    inputs_all, outgrad_all = both[:, :width], both[:, width:]
    preact = jnp.dot(inputs_all, w_in, preferred_element_type=F32).astype(BF16)
    back = contract_cols(outgrad_all, w_out).astype(BF16)
    sums = sum_model(jnp.concatenate([preact, back], axis=1))
    activation, grad_pre = activate(
        sums[:, :hidden] + b_in[None, :], sums[:, hidden:]
    )
    results = gather_blocks(jnp.concatenate([activation, grad_pre], axis=1), "x")
    activation, grad_pre = results[:, :hidden], results[:, hidden:]
    half = grad_pre.shape[0] // 2
    other = swap_cores(contract_cols(grad_pre[half:], w_in).astype(BF16))
    partial = contract_cols(grad_pre[:half], w_in) + other.astype(F32)
    grad_acts = sum_blocks(partial.astype(BF16), PLANE).astype(BF16)
    grad_w_in = contract_rows(inputs_all, grad_pre).astype(BF16)
    grad_b_in = jnp.sum(grad_pre.astype(F32), axis=0)
    grad_w_out = contract_rows(activation, outgrad_all).astype(BF16)
    return (grad_acts, grad_w_in, grad_b_in, grad_w_out)


def solution(mesh):
    fine = Mesh(mesh.devices.reshape(8, 4, 2, 2, 4), ("y", "zl", "co", "zh", "x"))
    tokens = ("y", "zl", "co")
    return jax.shard_map(
        body,
        mesh=fine,
        in_specs=(
            P(tokens, MODEL),
            P(tokens, MODEL),
            P(MODEL, tokens),
            P(tokens),
            P(tokens, MODEL),
        ),
        out_specs=(
            P(tokens, MODEL),
            P(MODEL, tokens),
            P(tokens),
            P(tokens, MODEL),
        ),
        check_vma=False,
    )
```

```python
import jax
import jax.numpy as jnp
from jax import lax
from jax.experimental import pallas as pl
from jax.experimental.pallas import tpu as pltpu
from jax.sharding import Mesh, PartitionSpec as P

BF16 = jnp.bfloat16
F32 = jnp.float32
PLANE = ("y", "zl")
MODEL = ("zh", "x")


def activate(preact, back):
    cdf = 0.5 * (1.0 + lax.erf(preact * 0.7071067811865476))
    dens = jnp.exp(-0.5 * preact * preact) * 0.3989422804014327
    activation = (preact * cdf).astype(BF16)
    grad_pre = (back * (cdf + preact * dens)).astype(BF16)
    return activation, grad_pre


def contract_rows(left, right):
    return lax.dot_general(
        left, right, (((0,), (0,)), ((), ())), preferred_element_type=F32
    )


def contract_cols(left, right):
    return lax.dot_general(
        left, right, (((1,), (1,)), ((), ())), preferred_element_type=F32
    )


IN_VMEM = pl.BlockSpec(memory_space=pltpu.VMEM)
IN_HBM = pl.BlockSpec(memory_space=pltpu.HBM)
COMPILER = pltpu.CompilerParams(vmem_limit_bytes=16 * 1024 * 1024)


def call(kernel, shape, operands, specs, scratch=(), flops=0):
    moved = sum(o.size * o.dtype.itemsize for o in operands)
    return pl.pallas_call(
        kernel,
        out_shape=jax.ShapeDtypeStruct(shape, BF16),
        in_specs=specs,
        out_specs=IN_VMEM,
        scratch_shapes=list(scratch),
        compiler_params=COMPILER,
        cost_estimate=pl.CostEstimate(
            flops=flops, bytes_accessed=moved, transcendentals=0
        ),
    )(*operands)


def stage_kernel(value, out):
    out[...] = value[...]


def stage(value):
    return call(stage_kernel, value.shape, (value,), [IN_VMEM])


def hidden_kernel(tokens, *refs):
    weights, out = refs[:4], refs[4]
    width, hidden = weights[0].shape
    for i, weight in enumerate(weights):
        if i < 2:
            term = jnp.dot(tokens[:, :width], weight[...], preferred_element_type=F32)
        else:
            term = contract_cols(tokens[:, width:], weight[...])
        out[:, i * hidden : (i + 1) * hidden] = term.astype(BF16)


def hidden_terms(tokens, weights):
    rows, hidden = tokens.shape[0], weights[0].shape[1]
    return call(
        hidden_kernel,
        (rows, 4 * hidden),
        (tokens, *weights),
        [IN_VMEM] * 5,
        flops=2 * rows * sum(w.size for w in weights),
    )


def inputs_kernel(results, own, other, out):
    hidden = own.shape[1]
    term = contract_cols(results[:, 2 * hidden : 3 * hidden], own[...])
    term += contract_cols(results[:, 3 * hidden :], other[...])
    out[...] = term.astype(BF16)


def inputs_term(results, weights):
    rows, width = results.shape[0], weights[0].shape[0]
    return call(
        inputs_kernel,
        (rows, width),
        (results, *weights),
        [IN_VMEM] * 3,
        flops=2 * rows * sum(w.size for w in weights),
    )


def activate_kernel(mine, other, bias, out):
    half = bias.shape[1]
    sums = mine[...].astype(F32) + other[...].astype(F32)
    activation, grad_pre = activate(sums[:, :half] + bias[...], sums[:, half:])
    for i in range(out.shape[0]):
        out[i, :, :half] = activation
        out[i, :, half:] = grad_pre


def sum_kernel(blocks, out):
    total = blocks[0].astype(F32)
    for i in range(1, blocks.shape[0]):
        total += blocks[i].astype(F32)
    out[...] = total.astype(BF16)


def exchange(blocks, axes):
    return lax.all_to_all(blocks, axes, 0, 0, tiled=True)


def sum_exchanged(value, axes):
    count = lax.axis_size(axes)
    rows, columns = value.shape[0] // count, value.shape[1]
    blocks = exchange(value.reshape(count, rows, columns), axes)
    return call(sum_kernel, (rows, columns), (blocks,), [IN_VMEM])


def swap_cores(value):
    return jax.tree.map(lambda v: lax.ppermute(v, "co", [(0, 1), (1, 0)]), value)


def body(acts, grad_out, w_in, b_in, w_out):
    width, hidden = w_in.shape
    others = swap_cores((w_in, w_out, b_in))
    staged = stage(w_in), stage(w_out)
    pair = jnp.concatenate([acts, grad_out], axis=1)
    copies = jnp.broadcast_to(pair[None], (lax.axis_size(PLANE), *pair.shape))
    tokens = exchange(copies, PLANE).reshape(-1, 2 * width)
    tokens, (w_in_other, w_out_other, b_in_other), (w_in, w_out) = (
        lax.optimization_barrier((tokens, others, staged))
    )
    terms = hidden_terms(tokens, (w_in, w_in_other, w_out, w_out_other))
    mine = sum_exchanged(terms, "x")
    other = lax.ppermute(mine, "zh", [(0, 1), (1, 0)])
    bias = jnp.concatenate([b_in, b_in_other])[None, :]
    copies = call(
        activate_kernel,
        (lax.axis_size("x"), *mine.shape),
        (mine, other, bias),
        [IN_VMEM] * 3,
    )
    results = exchange(copies, "x").reshape(-1, 4 * hidden)
    grad_acts = sum_exchanged(inputs_term(results, (w_in, w_in_other)), PLANE)

    inputs, outgrad = tokens[:, :width], tokens[:, width:]
    activation, grad_pre = results[:, : 2 * hidden], results[:, 2 * hidden :]
    tokens_other, activation_other, grad_pre_other = swap_cores(
        (tokens, activation[:, hidden:], grad_pre[:, hidden:])
    )
    inputs_all = jnp.concatenate([inputs, tokens_other[:, :width]], axis=0)
    outgrad_all = jnp.concatenate([outgrad, tokens_other[:, width:]], axis=0)
    activation = jnp.concatenate([activation[:, :hidden], activation_other], axis=0)
    grad_pre = jnp.concatenate([grad_pre[:, :hidden], grad_pre_other], axis=0)
    grad_w_in = contract_rows(inputs_all, grad_pre).astype(BF16)
    grad_b_in = jnp.sum(grad_pre.astype(F32), axis=0)
    grad_w_out = contract_rows(activation, outgrad_all).astype(BF16)
    return (grad_acts, grad_w_in, grad_b_in, grad_w_out)


def solution(mesh):
    fine = Mesh(mesh.devices.reshape(8, 4, 2, 2, 4), ("y", "zl", "co", "zh", "x"))
    tokens = ("y", "zl", "co")
    return jax.shard_map(
        body,
        mesh=fine,
        in_specs=(
            P(tokens, MODEL),
            P(tokens, MODEL),
            P(MODEL, tokens),
            P(tokens),
            P(tokens, MODEL),
        ),
        out_specs=(
            P(tokens, MODEL),
            P(MODEL, tokens),
            P(tokens),
            P(tokens, MODEL),
        ),
        check_vma=False,
    )
```

```python
import jax
import jax.numpy as jnp
from jax import lax
from jax.experimental import pallas as pl
from jax.experimental.pallas import tpu as pltpu
from jax.sharding import Mesh, PartitionSpec as P

BF16 = jnp.bfloat16
F32 = jnp.float32
PLANE = ("y", "zl")
MODEL = ("zh", "x")


def activate(preact, back):
    cdf = 0.5 * (1.0 + lax.erf(preact * 0.7071067811865476))
    dens = jnp.exp(-0.5 * preact * preact) * 0.3989422804014327
    activation = (preact * cdf).astype(BF16)
    grad_pre = (back * (cdf + preact * dens)).astype(BF16)
    return activation, grad_pre


def contract_rows(left, right):
    return lax.dot_general(
        left, right, (((0,), (0,)), ((), ())), preferred_element_type=F32
    )


def contract_cols(left, right):
    return lax.dot_general(
        left, right, (((1,), (1,)), ((), ())), preferred_element_type=F32
    )


IN_VMEM = pl.BlockSpec(memory_space=pltpu.VMEM)
IN_HBM = pl.BlockSpec(memory_space=pltpu.HBM)
COMPILER = pltpu.CompilerParams(vmem_limit_bytes=16 * 1024 * 1024)


def call(kernel, shape, operands, specs, scratch=(), flops=0):
    moved = sum(o.size * o.dtype.itemsize for o in operands)
    return pl.pallas_call(
        kernel,
        out_shape=jax.ShapeDtypeStruct(shape, BF16),
        in_specs=specs,
        out_specs=IN_VMEM,
        scratch_shapes=list(scratch),
        compiler_params=COMPILER,
        cost_estimate=pl.CostEstimate(
            flops=flops, bytes_accessed=moved, transcendentals=0
        ),
    )(*operands)


def stage_kernel(value, out):
    out[...] = value[...]


def stage(value):
    return call(stage_kernel, value.shape, (value,), [IN_VMEM])


def preact_kernel(tokens, weight, out):
    term = jnp.dot(
        tokens[:, : weight.shape[0]], weight[...], preferred_element_type=F32
    )
    out[...] = term.astype(BF16)


def back_kernel(tokens, weight, out):
    term = contract_cols(tokens[:, weight.shape[1] :], weight[...])
    out[...] = term.astype(BF16)


def last_kernel(tokens, weight, *refs):
    earlier, out = refs[:-1], refs[-1]
    hidden = weight.shape[0]
    for i, ref in enumerate(earlier):
        out[:, i * hidden : (i + 1) * hidden] = ref[...]
    term = contract_cols(tokens[:, weight.shape[1] :], weight[...])
    out[:, len(earlier) * hidden :] = term.astype(BF16)


def hidden_terms(tokens, weights):
    rows, hidden = tokens.shape[0], weights[0].shape[1]
    terms = []
    for i, weight in enumerate(weights):
        last = i == 3
        terms.append(
            call(
                last_kernel if last else preact_kernel if i < 2 else back_kernel,
                (rows, 4 * hidden if last else hidden),
                (tokens, weight, *(terms if last else ())),
                [IN_VMEM] * (5 if last else 2),
                flops=2 * rows * weight.size,
            )
        )
    return terms[-1]


def inputs_kernel(results, own, other, out):
    hidden = own.shape[1]
    term = contract_cols(results[:, 2 * hidden : 3 * hidden], own[...])
    term += contract_cols(results[:, 3 * hidden :], other[...])
    out[...] = term.astype(BF16)


def inputs_term(results, weights):
    rows, width = results.shape[0], weights[0].shape[0]
    return call(
        inputs_kernel,
        (rows, width),
        (results, *weights),
        [IN_VMEM] * 3,
        flops=2 * rows * sum(w.size for w in weights),
    )


def activate_kernel(mine, other, bias, out):
    half = bias.shape[1]
    sums = mine[...].astype(F32) + other[...].astype(F32)
    activation, grad_pre = activate(sums[:, :half] + bias[...], sums[:, half:])
    for i in range(out.shape[0]):
        out[i, :, :half] = activation
        out[i, :, half:] = grad_pre


def sum_kernel(blocks, out):
    total = blocks[0].astype(F32)
    for i in range(1, blocks.shape[0]):
        total += blocks[i].astype(F32)
    out[...] = total.astype(BF16)


def exchange(blocks, axes):
    return lax.all_to_all(blocks, axes, 0, 0, tiled=True)


def sum_exchanged(value, axes):
    count = lax.axis_size(axes)
    rows, columns = value.shape[0] // count, value.shape[1]
    blocks = exchange(value.reshape(count, rows, columns), axes)
    return call(sum_kernel, (rows, columns), (blocks,), [IN_VMEM])


def swap_cores(value):
    return jax.tree.map(lambda v: lax.ppermute(v, "co", [(0, 1), (1, 0)]), value)


def body(acts, grad_out, w_in, b_in, w_out):
    width, hidden = w_in.shape
    others = swap_cores((w_in, w_out, b_in))
    staged = stage(w_in), stage(w_out)
    pair = jnp.concatenate([acts, grad_out], axis=1)
    copies = jnp.broadcast_to(pair[None], (lax.axis_size(PLANE), *pair.shape))
    tokens = exchange(copies, PLANE).reshape(-1, 2 * width)
    tokens, (w_in_other, w_out_other, b_in_other), (w_in, w_out) = (
        lax.optimization_barrier((tokens, others, staged))
    )
    terms = hidden_terms(tokens, (w_in, w_in_other, w_out, w_out_other))
    mine = sum_exchanged(terms, "x")
    other = lax.ppermute(mine, "zh", [(0, 1), (1, 0)])
    bias = jnp.concatenate([b_in, b_in_other])[None, :]
    copies = call(
        activate_kernel,
        (lax.axis_size("x"), *mine.shape),
        (mine, other, bias),
        [IN_VMEM] * 3,
    )
    results = exchange(copies, "x").reshape(-1, 4 * hidden)
    grad_acts = sum_exchanged(inputs_term(results, (w_in, w_in_other)), PLANE)

    inputs, outgrad = tokens[:, :width], tokens[:, width:]
    activation, grad_pre = results[:, : 2 * hidden], results[:, 2 * hidden :]
    tokens_other, activation_other, grad_pre_other = swap_cores(
        (tokens, activation[:, hidden:], grad_pre[:, hidden:])
    )
    inputs_all = jnp.concatenate([inputs, tokens_other[:, :width]], axis=0)
    outgrad_all = jnp.concatenate([outgrad, tokens_other[:, width:]], axis=0)
    activation = jnp.concatenate([activation[:, :hidden], activation_other], axis=0)
    grad_pre = jnp.concatenate([grad_pre[:, :hidden], grad_pre_other], axis=0)
    grad_w_in = contract_rows(inputs_all, grad_pre).astype(BF16)
    grad_b_in = jnp.sum(grad_pre.astype(F32), axis=0)
    grad_w_out = contract_rows(activation, outgrad_all).astype(BF16)
    return (grad_acts, grad_w_in, grad_b_in, grad_w_out)


def solution(mesh):
    fine = Mesh(mesh.devices.reshape(8, 4, 2, 2, 4), ("y", "zl", "co", "zh", "x"))
    tokens = ("y", "zl", "co")
    return jax.shard_map(
        body,
        mesh=fine,
        in_specs=(
            P(tokens, MODEL),
            P(tokens, MODEL),
            P(MODEL, tokens),
            P(tokens),
            P(tokens, MODEL),
        ),
        out_specs=(
            P(tokens, MODEL),
            P(MODEL, tokens),
            P(tokens),
            P(tokens, MODEL),
        ),
        check_vma=False,
    )
```

```python
import jax
import jax.numpy as jnp
from jax import lax
from jax.experimental import pallas as pl
from jax.experimental.pallas import tpu as pltpu
from jax.sharding import Mesh, PartitionSpec as P

BF16 = jnp.bfloat16
F32 = jnp.float32
PLANE = "t"
ORDER = (
    19, 6, 9, 20, 24, 22, 27, 1, 10, 28, 3, 13, 2, 5, 18, 25, 23, 17, 7, 14, 31, 15,
    26, 0, 12, 4, 11, 29, 16, 21, 8, 30,
)
GROUPS = [[2 * place + core for place in ORDER] for core in range(2)]
MODEL = ("zh", "x")


def activate(preact, back):
    cdf = 0.5 * (1.0 + lax.erf(preact * 0.7071067811865476))
    dens = jnp.exp(-0.5 * preact * preact) * 0.3989422804014327
    activation = (preact * cdf).astype(BF16)
    grad_pre = (back * (cdf + preact * dens)).astype(BF16)
    return activation, grad_pre


def contract_rows(left, right):
    return lax.dot_general(
        left, right, (((0,), (0,)), ((), ())), preferred_element_type=F32
    )


def contract_cols(left, right):
    return lax.dot_general(
        left, right, (((1,), (1,)), ((), ())), preferred_element_type=F32
    )


IN_VMEM = pl.BlockSpec(memory_space=pltpu.VMEM)
IN_HBM = pl.BlockSpec(memory_space=pltpu.HBM)
COMPILER = pltpu.CompilerParams(vmem_limit_bytes=16 * 1024 * 1024)


def call(kernel, shape, operands, specs, scratch=(), flops=0):
    moved = sum(o.size * o.dtype.itemsize for o in operands)
    return pl.pallas_call(
        kernel,
        out_shape=jax.ShapeDtypeStruct(shape, BF16),
        in_specs=specs,
        out_specs=IN_VMEM,
        scratch_shapes=list(scratch),
        compiler_params=COMPILER,
        cost_estimate=pl.CostEstimate(
            flops=flops, bytes_accessed=moved, transcendentals=0
        ),
    )(*operands)


def stage_kernel(value, out):
    out[...] = value[...]


def stage(value):
    return call(stage_kernel, value.shape, (value,), [IN_VMEM])


def preact_kernel(tokens, weight, out):
    term = jnp.dot(
        tokens[:, : weight.shape[0]], weight[...], preferred_element_type=F32
    )
    out[...] = term.astype(BF16)


def back_kernel(tokens, weight, out):
    term = contract_cols(tokens[:, weight.shape[1] :], weight[...])
    out[...] = term.astype(BF16)


def last_kernel(tokens, weight, *refs):
    earlier, out = refs[:-1], refs[-1]
    hidden = weight.shape[0]
    for i, ref in enumerate(earlier):
        out[:, i * hidden : (i + 1) * hidden] = ref[...]
    term = contract_cols(tokens[:, weight.shape[1] :], weight[...])
    out[:, len(earlier) * hidden :] = term.astype(BF16)


def hidden_terms(tokens, weights):
    rows, hidden = tokens.shape[0], weights[0].shape[1]
    terms = []
    for i, weight in enumerate(weights):
        last = i == 3
        terms.append(
            call(
                last_kernel if last else preact_kernel if i < 2 else back_kernel,
                (rows, 4 * hidden if last else hidden),
                (tokens, weight, *(terms if last else ())),
                [IN_VMEM] * (5 if last else 2),
                flops=2 * rows * weight.size,
            )
        )
    return terms[-1]


def inputs_kernel(results, own, other, out):
    hidden = own.shape[1]
    term = contract_cols(results[:, 2 * hidden : 3 * hidden], own[...])
    term += contract_cols(results[:, 3 * hidden :], other[...])
    out[...] = term.astype(BF16)


def inputs_term(results, weights):
    rows, width = results.shape[0], weights[0].shape[0]
    return call(
        inputs_kernel,
        (rows, width),
        (results, *weights),
        [IN_VMEM] * 3,
        flops=2 * rows * sum(w.size for w in weights),
    )


def activate_kernel(mine, other, bias, out):
    half = bias.shape[1]
    sums = mine[...].astype(F32) + other[...].astype(F32)
    activation, grad_pre = activate(sums[:, :half] + bias[...], sums[:, half:])
    for i in range(out.shape[0]):
        out[i, :, :half] = activation
        out[i, :, half:] = grad_pre


def sum_kernel(blocks, out):
    total = blocks[0].astype(F32)
    for i in range(1, blocks.shape[0]):
        total += blocks[i].astype(F32)
    out[...] = total.astype(BF16)


def exchange(blocks, axes):
    groups = GROUPS if axes == PLANE else None
    return lax.all_to_all(blocks, axes, 0, 0, axis_index_groups=groups, tiled=True)


def sum_exchanged(value, axes):
    count = len(ORDER) if axes == PLANE else lax.axis_size(axes)
    rows, columns = value.shape[0] // count, value.shape[1]
    blocks = exchange(value.reshape(count, rows, columns), axes)
    return call(sum_kernel, (rows, columns), (blocks,), [IN_VMEM])


def swap_cores(value):
    return jax.tree.map(lambda v: lax.ppermute(v, PLANE, [(i, i ^ 1) for i in range(64)]), value)


def body(acts, grad_out, w_in, b_in, w_out):
    width, hidden = w_in.shape
    others = swap_cores((w_in, w_out, b_in))
    staged = stage(w_in), stage(w_out)
    pair = jnp.concatenate([acts, grad_out], axis=1)
    copies = jnp.broadcast_to(pair[None], (len(ORDER), *pair.shape))
    tokens = exchange(copies, PLANE).reshape(-1, 2 * width)
    tokens, (w_in_other, w_out_other, b_in_other), (w_in, w_out) = (
        lax.optimization_barrier((tokens, others, staged))
    )
    terms = hidden_terms(tokens, (w_in, w_in_other, w_out, w_out_other))
    mine = sum_exchanged(terms, "x")
    other = lax.ppermute(mine, "zh", [(0, 1), (1, 0)])
    bias = jnp.concatenate([b_in, b_in_other])[None, :]
    copies = call(
        activate_kernel,
        (lax.axis_size("x"), *mine.shape),
        (mine, other, bias),
        [IN_VMEM] * 3,
    )
    results = exchange(copies, "x").reshape(-1, 4 * hidden)
    grad_acts = sum_exchanged(inputs_term(results, (w_in, w_in_other)), PLANE)

    inputs, outgrad = tokens[:, :width], tokens[:, width:]
    activation, grad_pre = results[:, : 2 * hidden], results[:, 2 * hidden :]
    tokens_other, activation_other, grad_pre_other = swap_cores(
        (tokens, activation[:, hidden:], grad_pre[:, hidden:])
    )
    inputs_all = jnp.concatenate([inputs, tokens_other[:, :width]], axis=0)
    outgrad_all = jnp.concatenate([outgrad, tokens_other[:, width:]], axis=0)
    activation = jnp.concatenate([activation[:, :hidden], activation_other], axis=0)
    grad_pre = jnp.concatenate([grad_pre[:, :hidden], grad_pre_other], axis=0)
    grad_w_in = contract_rows(inputs_all, grad_pre).astype(BF16)
    grad_b_in = jnp.sum(grad_pre.astype(F32), axis=0)
    grad_w_out = contract_rows(activation, outgrad_all).astype(BF16)
    return (grad_acts, grad_w_in, grad_b_in, grad_w_out)


def solution(mesh):
    fine = Mesh(mesh.devices.reshape(64, 2, 4), ("t", "zh", "x"))
    tokens = "t"
    return jax.shard_map(
        body,
        mesh=fine,
        in_specs=(
            P(tokens, MODEL),
            P(tokens, MODEL),
            P(MODEL, tokens),
            P(tokens),
            P(tokens, MODEL),
        ),
        out_specs=(
            P(tokens, MODEL),
            P(MODEL, tokens),
            P(tokens),
            P(tokens, MODEL),
        ),
        check_vma=False,
    )
```

```python
import jax
import jax.numpy as jnp
from jax import lax
from jax.experimental import pallas as pl
from jax.experimental.pallas import tpu as pltpu
from jax.sharding import Mesh, PartitionSpec as P

BF16 = jnp.bfloat16
F32 = jnp.float32
PLANE = "t"
ORDER = (
    31, 23, 18, 4, 12, 21, 8, 19, 28, 3, 2, 1, 24, 26, 14, 11, 17, 0, 7, 27, 29, 5,
    16, 25, 6, 15, 9, 20, 30, 22, 13, 10,
)
GROUPS = [[2 * place + core for place in ORDER] for core in range(2)]
MODEL = ("zh", "x")


def activate(preact, back):
    cdf = 0.5 * (1.0 + lax.erf(preact * 0.7071067811865476))
    dens = jnp.exp(-0.5 * preact * preact) * 0.3989422804014327
    activation = (preact * cdf).astype(BF16)
    grad_pre = (back * (cdf + preact * dens)).astype(BF16)
    return activation, grad_pre


def contract_rows(left, right):
    return lax.dot_general(
        left, right, (((0,), (0,)), ((), ())), preferred_element_type=F32
    )


def contract_cols(left, right):
    return lax.dot_general(
        left, right, (((1,), (1,)), ((), ())), preferred_element_type=F32
    )


IN_VMEM = pl.BlockSpec(memory_space=pltpu.VMEM)
IN_HBM = pl.BlockSpec(memory_space=pltpu.HBM)
COMPILER = pltpu.CompilerParams(vmem_limit_bytes=16 * 1024 * 1024)


def call(kernel, shape, operands, specs, scratch=(), flops=0):
    moved = sum(o.size * o.dtype.itemsize for o in operands)
    return pl.pallas_call(
        kernel,
        out_shape=jax.ShapeDtypeStruct(shape, BF16),
        in_specs=specs,
        out_specs=IN_VMEM,
        scratch_shapes=list(scratch),
        compiler_params=COMPILER,
        cost_estimate=pl.CostEstimate(
            flops=flops, bytes_accessed=moved, transcendentals=0
        ),
    )(*operands)


def stage_kernel(value, out):
    out[...] = value[...]


def stage(value):
    return call(stage_kernel, value.shape, (value,), [IN_VMEM])


def preact_kernel(tokens, weight, out):
    term = jnp.dot(
        tokens[:, : weight.shape[0]], weight[...], preferred_element_type=F32
    )
    out[...] = term.astype(BF16)


def back_kernel(tokens, weight, out):
    term = contract_cols(tokens[:, weight.shape[1] :], weight[...])
    out[...] = term.astype(BF16)


def last_kernel(tokens, weight, *refs):
    earlier, out = refs[:-1], refs[-1]
    hidden = weight.shape[0]
    for i, ref in enumerate(earlier):
        out[:, i * hidden : (i + 1) * hidden] = ref[...]
    term = contract_cols(tokens[:, weight.shape[1] :], weight[...])
    out[:, len(earlier) * hidden :] = term.astype(BF16)


def hidden_terms(tokens, weights):
    rows, hidden = tokens.shape[0], weights[0].shape[1]
    terms = []
    for i, weight in enumerate(weights):
        last = i == 3
        terms.append(
            call(
                last_kernel if last else preact_kernel if i < 2 else back_kernel,
                (rows, 4 * hidden if last else hidden),
                (tokens, weight, *(terms if last else ())),
                [IN_VMEM] * (5 if last else 2),
                flops=2 * rows * weight.size,
            )
        )
    return terms[-1]


def inputs_kernel(results, own, other, out):
    hidden = own.shape[1]
    term = contract_cols(results[:, 2 * hidden : 3 * hidden], own[...])
    term += contract_cols(results[:, 3 * hidden :], other[...])
    out[...] = term.astype(BF16)


def inputs_term(results, weights):
    rows, width = results.shape[0], weights[0].shape[0]
    return call(
        inputs_kernel,
        (rows, width),
        (results, *weights),
        [IN_VMEM] * 3,
        flops=2 * rows * sum(w.size for w in weights),
    )


def activate_kernel(mine, other, bias, out):
    half = bias.shape[1]
    sums = mine[...].astype(F32) + other[...].astype(F32)
    activation, grad_pre = activate(sums[:, :half] + bias[...], sums[:, half:])
    for i in range(out.shape[0]):
        out[i, :, :half] = activation
        out[i, :, half:] = grad_pre


def sum_kernel(blocks, out):
    total = blocks[0].astype(F32)
    for i in range(1, blocks.shape[0]):
        total += blocks[i].astype(F32)
    out[...] = total.astype(BF16)


def exchange(blocks, axes):
    groups = GROUPS if axes == PLANE else None
    return lax.all_to_all(blocks, axes, 0, 0, axis_index_groups=groups, tiled=True)


def sum_exchanged(value, axes):
    count = len(ORDER) if axes == PLANE else lax.axis_size(axes)
    rows, columns = value.shape[0] // count, value.shape[1]
    blocks = exchange(value.reshape(count, rows, columns), axes)
    return call(sum_kernel, (rows, columns), (blocks,), [IN_VMEM])


def swap_cores(value):
    return jax.tree.map(lambda v: lax.ppermute(v, PLANE, [(i, i ^ 1) for i in range(64)]), value)


def body(acts, grad_out, w_in, b_in, w_out):
    width, hidden = w_in.shape
    others = swap_cores((w_in, w_out, b_in))
    staged = stage(w_in), stage(w_out)
    pair = jnp.concatenate([acts, grad_out], axis=1)
    copies = jnp.broadcast_to(pair[None], (len(ORDER), *pair.shape))
    tokens = exchange(copies, PLANE).reshape(-1, 2 * width)
    tokens, (w_in_other, w_out_other, b_in_other), (w_in, w_out) = (
        lax.optimization_barrier((tokens, others, staged))
    )
    terms = hidden_terms(tokens, (w_in, w_in_other, w_out, w_out_other))
    mine = sum_exchanged(terms, "x")
    other = lax.ppermute(mine, "zh", [(0, 1), (1, 0)])
    bias = jnp.concatenate([b_in, b_in_other])[None, :]
    copies = call(
        activate_kernel,
        (lax.axis_size("x"), *mine.shape),
        (mine, other, bias),
        [IN_VMEM] * 3,
    )
    results = exchange(copies, "x").reshape(-1, 4 * hidden)
    grad_acts = sum_exchanged(inputs_term(results, (w_in, w_in_other)), PLANE)

    inputs, outgrad = tokens[:, :width], tokens[:, width:]
    activation, grad_pre = results[:, : 2 * hidden], results[:, 2 * hidden :]
    tokens_other, activation_other, grad_pre_other = swap_cores(
        (tokens, activation[:, hidden:], grad_pre[:, hidden:])
    )
    inputs_all = jnp.concatenate([inputs, tokens_other[:, :width]], axis=0)
    outgrad_all = jnp.concatenate([outgrad, tokens_other[:, width:]], axis=0)
    activation = jnp.concatenate([activation[:, :hidden], activation_other], axis=0)
    grad_pre = jnp.concatenate([grad_pre[:, :hidden], grad_pre_other], axis=0)
    grad_w_in = contract_rows(inputs_all, grad_pre).astype(BF16)
    grad_b_in = jnp.sum(grad_pre.astype(F32), axis=0)
    grad_w_out = contract_rows(activation, outgrad_all).astype(BF16)
    return (grad_acts, grad_w_in, grad_b_in, grad_w_out)


def solution(mesh):
    fine = Mesh(mesh.devices.reshape(64, 2, 4), ("t", "zh", "x"))
    tokens = "t"
    return jax.shard_map(
        body,
        mesh=fine,
        in_specs=(
            P(tokens, MODEL),
            P(tokens, MODEL),
            P(MODEL, tokens),
            P(tokens),
            P(tokens, MODEL),
        ),
        out_specs=(
            P(tokens, MODEL),
            P(MODEL, tokens),
            P(tokens),
            P(tokens, MODEL),
        ),
        check_vma=False,
    )
```
